32 devices in a mesh: tm: 8 (over y, x, core), inner: 4 (over z).
Axes of the slice: x: 2, y: 2, z: 4, core: 2. Of those that a mesh axis runs over, the one named last changes fastest.
Arguments:
- query_input: bfloat16 [4096, 1792], P(('tm', 'inner')), may hold values from -6 to 6
- key_input: bfloat16 [4096, 1792], P(('tm', 'inner')), may hold values from -6 to 6
- value_input: bfloat16 [4096, 1792], P(('tm', 'inner')), may hold values from -6 to 6
- cotangent: bfloat16 [4096, 1792], P(('tm', 'inner')), may hold values from -6 to 6
- span_labels: int32 [4096], P(('tm', 'inner')), may hold values from 0 to 6, as said below
Outputs:
- query_gradient: bfloat16 [4096, 1792], P(('tm', 'inner'))
- key_gradient: bfloat16 [4096, 1792], P(('tm', 'inner'))
- value_gradient: bfloat16 [4096, 1792], P(('tm', 'inner'))
The draws below stay inside these ranges and needn't reach their ends.
Inputs may be any that keep to these rules, and one draw needn't show every extreme that they name: `span_labels`: span labels never fall along the tokens; each of the 7 spans holds 1 to 8 whole frames of 128 tokens and begins at a multiple of 128; one span holds exactly 1024 tokens.
All inputs are finite; a program needn't handle non-finite values.
Results may differ from the reference program's by a relative error of at most 0.008.
Values may be sent and summed in bfloat16 or wider, within the bound.
A program may use at most 192 MiB of HBM per device.

```python
import jax
import jax.numpy as jnp
from jax import lax

HEADS = 16
DH = 112
SPANS = 7
TOKENS = 4096
FRAME = 128


def draw_span_labels(key, part):
    first_key, second_key = jax.random.split(key)
    largest_slot = jax.random.randint(first_key, (), 0, SPANS)
    others = jnp.full((SPANS - 1,), 4, jnp.int32)
    move_keys = jax.random.split(second_key, 12)
    for step in range(12):
        picked = jax.random.randint(move_keys[step], (2,), 0, SPANS - 1)
        source = picked[0]
        target = picked[1]
        allowed = (source != target) & (others[source] > 1) & (others[target] < 8)
        amount = allowed.astype(jnp.int32)
        others = others.at[source].add(-amount)
        others = others.at[target].add(amount)
    positions = jnp.arange(SPANS, dtype=jnp.int32)
    shifted = jnp.clip(jnp.where(positions < largest_slot, positions, positions - 1), 0, SPANS - 2)
    lengths = jnp.where(positions == largest_slot, 8, others[shifted])
    bounds = jnp.cumsum(lengths)
    frames = jnp.arange(32, dtype=jnp.int32)
    frame_label = jnp.sum((frames[:, None] >= bounds[None, :-1]).astype(jnp.int32), axis=1)
    return jnp.repeat(frame_label, FRAME, total_repeat_length=32 * FRAME).astype(jnp.int32)


def block_scale(rng, dims, cuts, least, high):
    def one(position, parts):
        heights = jax.random.uniform(jax.random.fold_in(jax.random.fold_in(rng, 6), position), (parts,), jnp.float32, least / len(cuts), high / len(cuts))
        return jnp.repeat(jnp.exp(heights), dims[position] // parts).reshape((-1,) + (1,) * (len(dims) - position - 1))

    gain = one(*cuts[0])
    for cut in cuts[1:]:
        gain = gain * one(*cut)
    return gain


def normal_values(key, extent, width, most, cuts=(), kind=jnp.bfloat16):
    drawn = jax.random.normal(key, extent, jnp.float32) * width
    if len(cuts) > 0:
        drawn = block_scale(key, extent, cuts, -0.22, 0.18) * drawn
    return jnp.clip(drawn, min=-most, max=most).astype(kind)


def setup_inputs(seed: int = 0) -> dict:
    streams_of = jax.random.split(jax.random.key(seed), 6)
    query_input = normal_values(streams_of[0], (TOKENS, HEADS * DH), 1.0, 6.0, ((0, 32),))
    key_input = normal_values(streams_of[1], (TOKENS, HEADS * DH), 1.0, 6.0, ((0, 32),))
    value_input = normal_values(streams_of[2], (TOKENS, HEADS * DH), 1.0, 6.0, ((0, 32),))
    cotangent = normal_values(streams_of[3], (TOKENS, HEADS * DH), 1.0, 6.0, ((0, 32),))
    span_labels = draw_span_labels(jax.random.fold_in(streams_of[5], 71), 0)
    return dict(query_input=query_input, key_input=key_input, value_input=value_input, cotangent=cotangent, span_labels=span_labels)


loss_scale = 1024.0
exact = lax.Precision.HIGHEST


def round_low(values_in):
    return lax.optimization_barrier(values_in.astype(jnp.bfloat16)).astype(jnp.float32)


def reverse_cumsum(pieces):
    return jnp.flip(jnp.cumsum(jnp.flip(pieces, 0), 0), 0)


def reference(query_input, key_input, value_input, cotangent, span_labels):
    token_count = query_input.shape[0]
    levels = jnp.arange(SPANS, dtype=jnp.int32)
    onehot = (span_labels[:, None] == levels[None, :]).astype(jnp.float32)

    def split_heads(flat):
        return jnp.transpose(flat.reshape(token_count, HEADS, DH), (1, 0, 2))

    def per_head(pieces):
        query_head, key_head, value_head, cot_head = pieces
        feat_query = jnp.maximum(query_head, 0).astype(jnp.float32)
        feat_key = jnp.maximum(key_head, 0).astype(jnp.float32)
        value_full = value_head.astype(jnp.float32)
        key_spread = onehot[:, :, None] * feat_key[:, None, :]
        state_part = jnp.einsum("tck,tv->ckv", key_spread, value_full, precision=exact)
        mass_part = jnp.einsum("tc,tk->ck", onehot, feat_key, precision=exact)
        state_low = round_low(jnp.cumsum(state_part, 0))
        mass_low = round_low(jnp.cumsum(mass_part, 0))
        query_spread = onehot[:, :, None] * feat_query[:, None, :]
        numerator = jnp.einsum("tck,ckv->tv", query_spread, state_low, precision=exact)
        weight = jnp.einsum("tck,ck->t", query_spread, mass_low, precision=exact)
        denominator = weight / DH + 1.0
        output = numerator / (DH * denominator[:, None])
        scaled = cot_head.astype(jnp.float32) * loss_scale
        numer_back = round_low(scaled / (DH * denominator[:, None]))
        weight_back = round_low(-jnp.sum(scaled * output, axis=-1) / (DH * denominator))
        adjoint_part = jnp.einsum("tck,tv->ckv", query_spread, numer_back, precision=exact)
        adjoint_mass = jnp.einsum("tck,t->ck", query_spread, weight_back, precision=exact)
        adjoint_low = round_low(reverse_cumsum(adjoint_part))
        adjoint_mass_low = round_low(reverse_cumsum(adjoint_mass))
        back_spread = onehot[:, :, None] * numer_back[:, None, :]
        query_feat = jnp.einsum("tcv,ckv->tk", back_spread, state_low, precision=exact)
        query_feat = query_feat + jnp.dot(onehot, mass_low, precision=exact) * weight_back[:, None]
        value_spread = onehot[:, :, None] * value_full[:, None, :]
        key_feat = jnp.einsum("tcv,ckv->tk", value_spread, adjoint_low, precision=exact)
        key_feat = key_feat + jnp.dot(onehot, adjoint_mass_low, precision=exact)
        value_back = jnp.einsum("tck,ckv->tv", key_spread, adjoint_low, precision=exact)
        query_back = jnp.where(query_head > 0, query_feat, 0.0).astype(jnp.bfloat16)
        key_back = jnp.where(key_head > 0, key_feat, 0.0).astype(jnp.bfloat16)
        return query_back, key_back, value_back.astype(jnp.bfloat16)

    results = lax.map(per_head, (split_heads(query_input), split_heads(key_input), split_heads(value_input), split_heads(cotangent)))

    def merge_heads(stacked):
        return jnp.transpose(stacked, (1, 0, 2)).reshape(token_count, HEADS * DH)

    return merge_heads(results[0]), merge_heads(results[1]), merge_heads(results[2])
```

```python
import functools

import jax
import jax.numpy as jnp
from jax import lax
from jax.experimental import pallas as pl
from jax.experimental.pallas import tpu as pltpu
from jax.sharding import PartitionSpec as P

DH = 112
LANES = 128
HALF = 64
LOSS_SCALE = 1024.0
MASS = DH
LABEL = DH + 1


def mm(a, b, ca, cb):
    return lax.dot_general(
        a, b, (((ca,), (cb,)), ((), ())), preferred_element_type=jnp.float32
    )


def kernel(
    n, inner, heads,
    q_ref, k_ref, v_ref, c_ref, lab_ref,
    dq_ref, dk_ref, dv_ref,
    qp, kp, vp, cp,
    s1, r1, o1, w1, s2, r2, o2, w2, cum,
    send_sem, recv_sem, back_sem1, back_sem2,
):
    units = 2 * heads
    ratio = n // units
    me = lax.axis_index("tm") * inner + lax.axis_index("inner")
    unit = me // ratio
    tokens = q_ref.shape[0]
    lane_t = lax.broadcasted_iota(jnp.int32, (tokens, LANES), 1)
    lane_h = lax.broadcasted_iota(jnp.int32, (HALF, LANES), 1)
    lane_s = lax.broadcasted_iota(jnp.int32, (LANES, LANES), 1)

    def place(d):
        return {"tm": d // inner, "inner": d % inner}

    def send(src, dst, d, ssem, rsem):
        pltpu.make_async_remote_copy(
            src_ref=src, dst_ref=dst, send_sem=ssem, recv_sem=rsem,
            device_id=place(d), device_id_type=pl.DeviceIdType.MESH,
        ).start()

    def drain(ref, sem):
        pltpu.make_async_copy(ref, ref, sem).wait()

    barrier = pltpu.get_barrier_semaphore()

    def greet(i, carry):
        pl.semaphore_signal(
            barrier, inc=1, device_id=place((me + i) % n),
            device_id_type=pl.DeviceIdType.MESH,
        )
        return carry

    lax.fori_loop(1, n, greet, 0)

    def scatter(src, dst, ssem, rsem):
        if ratio == 1:
            pltpu.make_async_copy(src.at[me], dst.at[me], rsem).start()

            def one(i, carry):
                u = (me + i) % units
                send(src.at[u], dst.at[me], u, ssem, rsem)
                return carry

            lax.fori_loop(1, units, one, 0)
        else:

            def one(i, carry):
                u = (unit + i) % units

                @pl.when(u * ratio == me)
                def _():
                    pltpu.make_async_copy(src.at[u], dst.at[me], rsem).start()

                @pl.when(u * ratio != me)
                def _():
                    send(src.at[u], dst.at[me], u * ratio, ssem, rsem)

                return carry

            lax.fori_loop(0, units, one, 0)

    def scatter_end(src, ssem):
        if ratio == 1:
            drain(src.at[pl.ds(0, units - 1)], ssem)
        else:

            @pl.when(me % ratio == 0)
            def _():
                drain(src.at[pl.ds(0, units - 1)], ssem)

            @pl.when(me % ratio != 0)
            def _():
                drain(src.at[pl.ds(0, units)], ssem)

    def as_owner(fn):
        if ratio == 1:
            fn()
        else:
            pl.when(me % ratio == 0)(fn)

    def visible(got, out, back, ssem, rsem, bsem, reverse):
        def work():
            drain(got, rsem)

            def add(i, acc):
                d = n - 1 - i if reverse else i
                acc = acc + got[d].astype(jnp.float32)
                cum[d] = acc
                return acc

            last = lax.fori_loop(
                0, n, add, jnp.zeros((HALF, LANES), jnp.float32), unroll=4
            )

            def label(d):
                return jnp.broadcast_to(
                    got[d][:, LABEL : LABEL + 1].astype(jnp.float32), (HALF, LANES)
                )

            def pick(i, carry):
                cur, lab = carry
                d = i if reverse else n - 1 - i
                here = label(d)
                cur = jnp.where(here == lab, cur, cum[d])
                out[d] = jnp.where(lane_h == LABEL, 0.0, cur).astype(jnp.bfloat16)
                return cur, here

            first = label(0 if reverse else n - 1)
            lax.fori_loop(0, n, pick, (last, first), unroll=4)
            pltpu.make_async_copy(out.at[me], back.at[unit], bsem.at[unit]).start()

            def one(i, carry):
                d = (me + i) % n
                send(out.at[d], back.at[unit], d, ssem, bsem.at[unit])
                return carry

            lax.fori_loop(1, n, one, 0)

        as_owner(work)

    zero = jnp.zeros((tokens, LANES), jnp.bfloat16)
    ones = jnp.where(lane_t == MASS, 1.0, 0.0).astype(jnp.bfloat16)
    for h in range(heads):
        cols = slice(h * DH, (h + 1) * DH)
        qp[h] = zero
        kp[h] = zero
        cp[h] = zero
        vp[h] = ones
        kp[h, :, :DH] = jnp.maximum(k_ref[:, cols], 0)
        vp[h, :, :DH] = v_ref[:, cols]
    lab = jnp.broadcast_to(lab_ref[...].astype(jnp.float32), (LANES, LANES))

    def stage(dst, h, state):
        state = jnp.where(lane_s == LABEL, lab, state).astype(jnp.bfloat16)
        dst[2 * h] = state[:HALF]
        dst[2 * h + 1] = state[HALF:]

    for h in range(heads):
        stage(s1, h, mm(kp[h], vp[h], 0, 0))

    pl.semaphore_wait(barrier, n - 1)
    scatter(s1, r1, send_sem.at[0], recv_sem.at[0])
    for h in range(heads):
        cols = slice(h * DH, (h + 1) * DH)
        qp[h, :, :DH] = jnp.maximum(q_ref[:, cols], 0)
        cp[h, :, :DH] = c_ref[:, cols]
    visible(r1, o1, w1, send_sem.at[1], recv_sem.at[0], back_sem1, False)

    for h in range(heads):
        drain(w1.at[2 * h], back_sem1.at[2 * h])
        drain(w1.at[2 * h + 1], back_sem1.at[2 * h + 1])
        state = w1[2 * h : 2 * h + 2].reshape(LANES, LANES)
        query = qp[h]
        both = mm(query, state, 1, 0)
        inv = 1.0 / (both[:, MASS : MASS + 1] + float(DH))
        cot = cp[h].astype(jnp.float32) * LOSS_SCALE
        dot = jnp.sum(cot * both, axis=1, keepdims=True)
        back = jnp.where(lane_t == MASS, -(dot * inv) * inv, cot * inv)
        back = back.astype(jnp.bfloat16)
        stage(s2, h, mm(query, back, 0, 0))
        grad = mm(back, state, 1, 1)
        grad = jnp.where(query.astype(jnp.float32) > 0, grad, 0.0)
        dq_ref[:, h * DH : (h + 1) * DH] = grad.astype(jnp.bfloat16)[:, :DH]

    scatter(s2, r2, send_sem.at[2], recv_sem.at[1])
    visible(r2, o2, w2, send_sem.at[3], recv_sem.at[1], back_sem2, True)

    for h in range(heads):
        drain(w2.at[2 * h], back_sem2.at[2 * h])
        drain(w2.at[2 * h + 1], back_sem2.at[2 * h + 1])
        adjoint = w2[2 * h : 2 * h + 2].reshape(LANES, LANES)
        key = kp[h]
        grad = mm(vp[h], adjoint, 1, 1)
        grad = jnp.where(key.astype(jnp.float32) > 0, grad, 0.0)
        dk_ref[:, h * DH : (h + 1) * DH] = grad.astype(jnp.bfloat16)[:, :DH]
        grad = mm(key, adjoint, 1, 0)
        dv_ref[:, h * DH : (h + 1) * DH] = grad.astype(jnp.bfloat16)[:, :DH]

    scatter_end(s1, send_sem.at[0])
    scatter_end(s2, send_sem.at[2])

    def finish():
        drain(o1.at[pl.ds(0, n - 1)], send_sem.at[1])
        drain(o2.at[pl.ds(0, n - 1)], send_sem.at[3])

    as_owner(finish)


def local(query, key, value, cotangent, labels):
    tokens, width = query.shape
    heads = width // DH
    inner = lax.axis_size("inner")
    n = lax.axis_size("tm") * inner
    units = 2 * heads
    vmem = pl.BlockSpec(memory_space=pltpu.VMEM)
    shape = jax.ShapeDtypeStruct((tokens, width), jnp.bfloat16)
    padded = pltpu.VMEM((heads, tokens, LANES), jnp.bfloat16)
    per_unit = pltpu.VMEM((units, HALF, LANES), jnp.bfloat16)
    per_device = pltpu.VMEM((n, HALF, LANES), jnp.bfloat16)
    flops = 12 * heads * tokens * DH * DH
    return pl.pallas_call(
        functools.partial(kernel, n, inner, heads),
        out_shape=(shape, shape, shape),
        in_specs=[vmem] * 5,
        out_specs=(vmem, vmem, vmem),
        scratch_shapes=[
            padded, padded, padded, padded,
            per_unit, per_device, per_device, per_unit,
            per_unit, per_device, per_device, per_unit,
            pltpu.VMEM((n, HALF, LANES), jnp.float32),
            pltpu.SemaphoreType.DMA((4,)),
            pltpu.SemaphoreType.DMA((2,)),
            pltpu.SemaphoreType.DMA((units,)),
            pltpu.SemaphoreType.DMA((units,)),
        ],
        compiler_params=pltpu.CompilerParams(
            collective_id=0, has_side_effects=True, vmem_limit_bytes=48 * 2**20
        ),
        cost_estimate=pl.CostEstimate(
            flops=flops, bytes_accessed=14 * tokens * width, transcendentals=0
        ),
    )(query, key, value, cotangent, labels[:LANES].reshape(1, LANES))


def solution(mesh):
    rows = P(("tm", "inner"), None)
    return jax.shard_map(
        local,
        mesh=mesh,
        in_specs=(rows, rows, rows, rows, P(("tm", "inner"))),
        out_specs=(rows, rows, rows),
        check_vma=False,
    )
```

```python
import functools

import jax
import jax.numpy as jnp
from jax import lax
from jax.experimental import pallas as pl
from jax.experimental.pallas import tpu as pltpu
from jax.sharding import PartitionSpec as P

DH = 112
LANES = 128
HALF = 64
LOSS_SCALE = 1024.0
MASS = DH
LABEL = DH + 1


def mm(a, b, ca, cb):
    return lax.dot_general(
        a, b, (((ca,), (cb,)), ((), ())), preferred_element_type=jnp.float32
    )


GROUPS = 4
ROWS = (HALF, DH - HALF)


def kernel(
    n, inner, heads,
    q_hbm, k_hbm, v_hbm, c_hbm, lab_hbm,
    dq_ref, dk_ref, dv_ref,
    q_ref, k_ref, v_ref, c_ref, lab_ref,
    qp, kp, vp, cp, nb,
    s1, r1, o1, w1, s2, r2, o2, w2, cum,
    in_sem, send_sem, out_sem, recv_sem, back_sem1, back_sem2,
):
    units = 2 * heads
    ratio = n // units
    me = lax.axis_index("tm") * inner + lax.axis_index("inner")
    unit = me // ratio
    per_group = units // GROUPS
    group = unit // per_group
    tokens = q_hbm.shape[0]
    lane_t = lax.broadcasted_iota(jnp.int32, (tokens, LANES), 1)
    lane_s = lax.broadcasted_iota(jnp.int32, (LANES, LANES), 1)

    def place(d):
        return {"tm": d // inner, "inner": d % inner}

    def send(src, dst, d, ssem, rsem):
        pltpu.make_async_remote_copy(
            src_ref=src, dst_ref=dst, send_sem=ssem, recv_sem=rsem,
            device_id=place(d), device_id_type=pl.DeviceIdType.MESH,
        ).start()

    def drain(ref, sem):
        pltpu.make_async_copy(ref, ref, sem).wait()

    fetch = [
        pltpu.make_async_copy(a, b, in_sem.at[i])
        for i, (a, b) in enumerate(
            (
                (lab_hbm, lab_ref), (k_hbm, k_ref), (v_hbm, v_ref),
                (q_hbm, q_ref), (c_hbm, c_ref),
            )
        )
    ]
    for copy in fetch:
        copy.start()

    barrier = pltpu.get_barrier_semaphore()

    def greet(i, carry):
        pl.semaphore_signal(
            barrier, inc=1, device_id=place((me + i) % n),
            device_id_type=pl.DeviceIdType.MESH,
        )
        return carry

    lax.fori_loop(1, n, greet, 0)

    def each_group(fn):
        def step(i, carry):
            now = (group + GROUPS - i) % GROUPS
            for g in range(GROUPS):
                pl.when(now == g)(functools.partial(fn, g))
            return carry

        lax.fori_loop(0, GROUPS, step, 0)

    def post(src, dst, g, ssem, rsem):
        pairs = per_group // 2

        def one(j, carry):
            pair = (unit // 2 + j) % pairs
            for b, rows in enumerate(ROWS):
                u = per_group * g + 2 * pair + b
                here = src.at[u, pl.ds(0, rows)]
                there = dst.at[me, pl.ds(0, rows)]

                @pl.when(u * ratio == me)
                def _():
                    pltpu.make_async_copy(here, there, rsem).start()

                @pl.when(u * ratio != me)
                def _():
                    send(here, there, u * ratio, ssem.at[b], rsem)

            return carry

        lax.fori_loop(0, pairs, one, 0)

    def as_owner(fn):
        for b, rows in enumerate(ROWS):
            mine = unit % 2 == b
            if ratio > 1:
                mine = mine & (me % ratio == 0)
            pl.when(mine)(functools.partial(fn, b, rows))

    def post_end(src, ssem):
        def owner(b, rows):
            for a, size in enumerate(ROWS):
                count = heads - 1 if a == b else heads
                drain(src.at[pl.ds(0, count), pl.ds(0, size)], ssem.at[a])

        as_owner(owner)
        if ratio > 1:

            @pl.when(me % ratio != 0)
            def _():
                for a, size in enumerate(ROWS):
                    drain(src.at[pl.ds(0, heads), pl.ds(0, size)], ssem.at[a])

    def visible(got, out, back, ssem, rsem, bsem, reverse):
        def work(b, rows):
            drain(got.at[pl.ds(0, n), pl.ds(0, rows)], rsem)
            lane_r = lax.broadcasted_iota(jnp.int32, (rows, LANES), 1)

            def add(i, acc):
                d = n - 1 - i if reverse else i
                acc = acc + got[d, :rows].astype(jnp.float32)
                cum[d, :rows] = acc
                return acc

            last = lax.fori_loop(
                0, n, add, jnp.zeros((rows, LANES), jnp.float32), unroll=4
            )

            def label(d):
                column = got[d, :16, LABEL : LABEL + 1].astype(jnp.float32)
                wide = jnp.broadcast_to(column, (16, LANES))
                return jnp.concatenate([wide] * (rows // 16), axis=0)

            def pick(i, carry):
                cur, lab = carry
                d = i if reverse else n - 1 - i
                here = label(d)
                cur = jnp.where(here == lab, cur, cum[d, :rows])
                out[d, :rows] = jnp.where(lane_r == LABEL, 0.0, cur).astype(
                    jnp.bfloat16
                )
                return cur, here

            first = label(0 if reverse else n - 1)
            lax.fori_loop(0, n, pick, (last, first), unroll=4)
            part = pl.ds(0, rows)
            there = back.at[unit, part]
            pltpu.make_async_copy(out.at[me, part], there, bsem.at[unit]).start()
            block = n // GROUPS

            def one(i, carry):
                d = block * ((me // block + i // block) % GROUPS) + (me + i) % block
                send(out.at[d, part], there, d, ssem, bsem.at[unit])
                return carry

            lax.fori_loop(1, n, one, 0)

        as_owner(work)

    def arrive(back, bsem, h):
        for b, rows in enumerate(ROWS):
            u = 2 * h + b
            drain(back.at[u, pl.ds(0, rows)], bsem.at[u])

    zero = jnp.zeros((tokens, LANES), jnp.bfloat16)
    ones = jnp.where(lane_t == MASS, 1.0, 0.0).astype(jnp.bfloat16)
    blank = jnp.zeros((HALF - ROWS[1], LANES), jnp.bfloat16)
    for h in range(heads):
        qp[h] = zero
        kp[h] = zero
        cp[h] = zero
        vp[h] = ones
        w1[2 * h + 1, ROWS[1] :] = blank
        w2[2 * h + 1, ROWS[1] :] = blank
    for copy in fetch[:3]:
        copy.wait()
    lab = jnp.broadcast_to(lab_ref[...].astype(jnp.float32), (LANES, LANES))

    def stage(dst, h, state):
        state = jnp.where(lane_s == LABEL, lab, state).astype(jnp.bfloat16)
        dst[2 * h] = state[:HALF]
        dst[2 * h + 1] = state[HALF:]

    def members(g):
        return range(g * heads // GROUPS, (g + 1) * heads // GROUPS)

    for h in range(heads):
        cols = slice(h * DH, (h + 1) * DH)
        kp[h, :, :DH] = jnp.maximum(k_ref[:, cols], 0)
        vp[h, :, :DH] = v_ref[:, cols]
    pl.semaphore_wait(barrier, n - 1)

    def keys(g):
        for h in members(g):
            stage(s1, h, mm(kp[h], vp[h], 0, 0))
        post(s1, r1, g, send_sem.at[0], recv_sem.at[0])

    each_group(keys)

    for copy in fetch[3:]:
        copy.wait()
    for h in range(heads):
        cols = slice(h * DH, (h + 1) * DH)
        qp[h, :, :DH] = jnp.maximum(q_ref[:, cols], 0)
        cp[h, :, :DH] = c_ref[:, cols]
    visible(r1, o1, w1, out_sem.at[0], recv_sem.at[0], back_sem1, False)

    def queries(g):
        for h in members(g):
            arrive(w1, back_sem1, h)
        for h in members(g):
            state = w1[2 * h : 2 * h + 2].reshape(LANES, LANES)
            query = qp[h]
            both = mm(query, state, 1, 0)
            inv = 1.0 / (both[:, MASS : MASS + 1] + float(DH))
            cot = cp[h].astype(jnp.float32) * LOSS_SCALE
            dot = jnp.sum(cot * both, axis=1, keepdims=True)
            back = jnp.where(lane_t == MASS, -(dot * inv) * inv, cot * inv)
            back = back.astype(jnp.bfloat16)
            nb[h] = back
            stage(s2, h, mm(query, back, 0, 0))
        post(s2, r2, g, send_sem.at[1], recv_sem.at[1])

    each_group(queries)

    for h in range(heads):
        state = w1[2 * h : 2 * h + 2].reshape(LANES, LANES)
        grad = mm(nb[h], state, 1, 1)
        grad = jnp.where(qp[h].astype(jnp.float32) > 0, grad, 0.0)
        dq_ref[:, h * DH : (h + 1) * DH] = grad.astype(jnp.bfloat16)[:, :DH]
    visible(r2, o2, w2, out_sem.at[1], recv_sem.at[1], back_sem2, True)

    def values(g):
        for h in members(g):
            arrive(w2, back_sem2, h)
        for h in members(g):
            adjoint = w2[2 * h : 2 * h + 2].reshape(LANES, LANES)
            key = kp[h]
            grad = mm(vp[h], adjoint, 1, 1)
            grad = jnp.where(key.astype(jnp.float32) > 0, grad, 0.0)
            dk_ref[:, h * DH : (h + 1) * DH] = grad.astype(jnp.bfloat16)[:, :DH]
            grad = mm(key, adjoint, 1, 0)
            dv_ref[:, h * DH : (h + 1) * DH] = grad.astype(jnp.bfloat16)[:, :DH]

    each_group(values)

    post_end(s1, send_sem.at[0])
    post_end(s2, send_sem.at[1])

    def finish(b, rows):
        drain(o1.at[pl.ds(0, n - 1), pl.ds(0, rows)], out_sem.at[0])
        drain(o2.at[pl.ds(0, n - 1), pl.ds(0, rows)], out_sem.at[1])

    as_owner(finish)


def local(query, key, value, cotangent, labels):
    tokens, width = query.shape
    heads = width // DH
    inner = lax.axis_size("inner")
    n = lax.axis_size("tm") * inner
    units = 2 * heads
    vmem = pl.BlockSpec(memory_space=pltpu.VMEM)
    shape = jax.ShapeDtypeStruct((tokens, width), jnp.bfloat16)
    padded = pltpu.VMEM((heads, tokens, LANES), jnp.bfloat16)
    flat = pltpu.VMEM((tokens, width), jnp.bfloat16)
    per_unit = pltpu.VMEM((units, HALF, LANES), jnp.bfloat16)
    per_device = pltpu.VMEM((n, HALF, LANES), jnp.bfloat16)
    flops = 12 * heads * tokens * DH * DH
    return pl.pallas_call(
        functools.partial(kernel, n, inner, heads),
        out_shape=(shape, shape, shape),
        in_specs=[pl.BlockSpec(memory_space=pltpu.HBM)] * 5,
        out_specs=(vmem, vmem, vmem),
        scratch_shapes=[
            flat, flat, flat, flat, pltpu.VMEM((1, LANES), jnp.int32),
            padded, padded, padded, padded, padded,
            per_unit, per_device, per_device, per_unit,
            per_unit, per_device, per_device, per_unit,
            pltpu.VMEM((n, HALF, LANES), jnp.float32),
            pltpu.SemaphoreType.DMA((5,)),
            pltpu.SemaphoreType.DMA((2, 2)),
            pltpu.SemaphoreType.DMA((2,)),
            pltpu.SemaphoreType.DMA((2,)),
            pltpu.SemaphoreType.DMA((units,)),
            pltpu.SemaphoreType.DMA((units,)),
        ],
        compiler_params=pltpu.CompilerParams(
            collective_id=0, has_side_effects=True, vmem_limit_bytes=63 * 2**20
        ),
        cost_estimate=pl.CostEstimate(
            flops=flops, bytes_accessed=14 * tokens * width, transcendentals=0
        ),
    )(query, key, value, cotangent, labels[:LANES].reshape(1, LANES))


def solution(mesh):
    rows = P(("tm", "inner"), None)
    return jax.shard_map(
        local,
        mesh=mesh,
        in_specs=(rows, rows, rows, rows, P(("tm", "inner"))),
        out_specs=(rows, rows, rows),
        check_vma=False,
    )
```

```python
import functools

import jax
import jax.numpy as jnp
from jax import lax
from jax.experimental import pallas as pl
from jax.experimental.pallas import tpu as pltpu
from jax.sharding import PartitionSpec as P

DH = 112
LANES = 128
HALF = 64
LOSS_SCALE = 1024.0
MASS = DH
LABEL = DH + 1


def mm(a, b, ca, cb):
    return lax.dot_general(
        a, b, (((ca,), (cb,)), ((), ())), preferred_element_type=jnp.float32
    )


GROUPS = 4
ROWS = (HALF, DH - HALF)


def kernel(
    n, inner, heads,
    q_hbm, k_hbm, v_hbm, c_hbm, lab_hbm,
    dq_ref, dk_ref, dv_ref,
    q_ref, k_ref, v_ref, c_ref, lab_ref,
    qp, kp, vp, cp, nb,
    s1, r1, o1, w1, s2, r2, o2, w2, cum,
    in_sem, send_sem, out_sem, recv_sem, back_sem1, back_sem2,
):
    units = 2 * heads
    ratio = n // units
    me = lax.axis_index("tm") * inner + lax.axis_index("inner")
    unit = me // ratio
    per_group = units // GROUPS
    group = unit // per_group
    tokens = q_hbm.shape[0]
    lane_t = lax.broadcasted_iota(jnp.int32, (tokens, LANES), 1)
    lane_s = lax.broadcasted_iota(jnp.int32, (LANES, LANES), 1)

    def place(d):
        return {"tm": d // inner, "inner": d % inner}

    def send(src, dst, d, ssem, rsem):
        pltpu.make_async_remote_copy(
            src_ref=src, dst_ref=dst, send_sem=ssem, recv_sem=rsem,
            device_id=place(d), device_id_type=pl.DeviceIdType.MESH,
        ).start()

    def drain(ref, sem):
        pltpu.make_async_copy(ref, ref, sem).wait()

    fetch = [
        pltpu.make_async_copy(a, b, in_sem.at[i])
        for i, (a, b) in enumerate(
            (
                (lab_hbm, lab_ref), (k_hbm, k_ref), (v_hbm, v_ref),
                (q_hbm, q_ref), (c_hbm, c_ref),
            )
        )
    ]
    for copy in fetch:
        copy.start()

    barrier = pltpu.get_barrier_semaphore()

    def greet(i, carry):
        pl.semaphore_signal(
            barrier, inc=1, device_id=place((me + i) % n),
            device_id_type=pl.DeviceIdType.MESH,
        )
        return carry

    lax.fori_loop(1, n, greet, 0)

    def each_group(fn):
        def step(i, carry):
            now = (group + GROUPS - i) % GROUPS
            for g in range(GROUPS):
                pl.when(now == g)(functools.partial(fn, g))
            return carry

        lax.fori_loop(0, GROUPS, step, 0)

    def post(src, dst, g, ssem, rsem):
        pairs = per_group // 2

        def one(j, carry):
            pair = (unit // 2 + j) % pairs
            for b, rows in enumerate(ROWS):
                u = per_group * g + 2 * pair + b
                here = src.at[u, pl.ds(0, rows)]
                there = dst.at[me, pl.ds(0, rows)]

                @pl.when(u * ratio == me)
                def _():
                    pltpu.make_async_copy(here, there, rsem).start()

                @pl.when(u * ratio != me)
                def _():
                    send(here, there, u * ratio, ssem.at[b], rsem)

            return carry

        lax.fori_loop(0, pairs, one, 0)

    def as_owner(fn):
        for b, rows in enumerate(ROWS):
            mine = unit % 2 == b
            if ratio > 1:
                mine = mine & (me % ratio == 0)
            pl.when(mine)(functools.partial(fn, b, rows))

    def post_end(src, ssem):
        def owner(b, rows):
            for a, size in enumerate(ROWS):
                count = heads - 1 if a == b else heads
                drain(src.at[pl.ds(0, count), pl.ds(0, size)], ssem.at[a])

        as_owner(owner)
        if ratio > 1:

            @pl.when(me % ratio != 0)
            def _():
                for a, size in enumerate(ROWS):
                    drain(src.at[pl.ds(0, heads), pl.ds(0, size)], ssem.at[a])

    def visible(got, out, back, ssem, rsem, bsem, reverse):
        def work(b, rows):
            drain(got.at[pl.ds(0, n), pl.ds(0, rows)], rsem)
            lane_r = lax.broadcasted_iota(jnp.int32, (rows, LANES), 1)

            def add(i, acc):
                d = n - 1 - i if reverse else i
                acc = acc + got[d, :rows].astype(jnp.float32)
                cum[d, :rows] = acc
                return acc

            last = lax.fori_loop(
                0, n, add, jnp.zeros((rows, LANES), jnp.float32), unroll=8
            )

            def label(d):
                column = got[d, :16, LABEL : LABEL + 1].astype(jnp.float32)
                wide = jnp.broadcast_to(column, (16, LANES))
                return jnp.concatenate([wide] * (rows // 16), axis=0)

            def pick(i, carry):
                cur, lab = carry
                d = i if reverse else n - 1 - i
                here = label(d)
                cur = jnp.where(here == lab, cur, cum[d, :rows])
                out[d, :rows] = jnp.where(lane_r == LABEL, 0.0, cur).astype(
                    jnp.bfloat16
                )
                return cur, here

            first = label(0 if reverse else n - 1)
            lax.fori_loop(0, n, pick, (last, first), unroll=8)
            part = pl.ds(0, rows)
            there = back.at[unit, part]
            pltpu.make_async_copy(out.at[me, part], there, bsem.at[unit]).start()
            block = n // GROUPS

            def one(i, carry):
                d = block * ((me // block + i // block) % GROUPS) + (me + i) % block
                send(out.at[d, part], there, d, ssem, bsem.at[unit])
                return carry

            lax.fori_loop(1, n, one, 0)

        as_owner(work)

    def arrive(back, bsem, h):
        for b, rows in enumerate(ROWS):
            u = 2 * h + b
            drain(back.at[u, pl.ds(0, rows)], bsem.at[u])

    zero = jnp.zeros((tokens, LANES), jnp.bfloat16)
    ones = jnp.where(lane_t == MASS, 1.0, 0.0).astype(jnp.bfloat16)
    blank = jnp.zeros((HALF - ROWS[1], LANES), jnp.bfloat16)
    for h in range(heads):
        qp[h] = zero
        kp[h] = zero
        cp[h] = zero
        vp[h] = ones
        w1[2 * h + 1, ROWS[1] :] = blank
        w2[2 * h + 1, ROWS[1] :] = blank
    for copy in fetch[:3]:
        copy.wait()
    lab = jnp.broadcast_to(lab_ref[...].astype(jnp.float32), (LANES, LANES))

    def stage(dst, h, state):
        state = jnp.where(lane_s == LABEL, lab, state).astype(jnp.bfloat16)
        dst[2 * h] = state[:HALF]
        dst[2 * h + 1] = state[HALF:]

    def members(g):
        return range(g * heads // GROUPS, (g + 1) * heads // GROUPS)

    pl.semaphore_wait(barrier, n - 1)

    def keys(g):
        for h in members(g):
            cols = slice(h * DH, (h + 1) * DH)
            kp[h, :, :DH] = jnp.maximum(k_ref[:, cols], 0)
            vp[h, :, :DH] = v_ref[:, cols]
        for h in members(g):
            stage(s1, h, mm(kp[h], vp[h], 0, 0))
        post(s1, r1, g, send_sem.at[0], recv_sem.at[0])

    each_group(keys)

    for copy in fetch[3:]:
        copy.wait()
    for h in range(heads):
        cols = slice(h * DH, (h + 1) * DH)
        qp[h, :, :DH] = jnp.maximum(q_ref[:, cols], 0)
        cp[h, :, :DH] = c_ref[:, cols]
    visible(r1, o1, w1, out_sem.at[0], recv_sem.at[0], back_sem1, False)

    def queries(g):
        for h in members(g):
            arrive(w1, back_sem1, h)
        for h in members(g):
            state = w1[2 * h : 2 * h + 2].reshape(LANES, LANES)
            query = qp[h]
            both = mm(query, state, 1, 0)
            inv = 1.0 / (both[:, MASS : MASS + 1] + float(DH))
            cot = cp[h].astype(jnp.float32) * LOSS_SCALE
            dot = jnp.sum(cot * both, axis=1, keepdims=True)
            back = jnp.where(lane_t == MASS, -(dot * inv) * inv, cot * inv)
            back = back.astype(jnp.bfloat16)
            nb[h] = back
            stage(s2, h, mm(query, back, 0, 0))
        post(s2, r2, g, send_sem.at[1], recv_sem.at[1])

    each_group(queries)

    for h in range(heads):
        state = w1[2 * h : 2 * h + 2].reshape(LANES, LANES)
        grad = mm(nb[h], state, 1, 1)
        grad = jnp.where(qp[h].astype(jnp.float32) > 0, grad, 0.0)
        dq_ref[:, h * DH : (h + 1) * DH] = grad.astype(jnp.bfloat16)[:, :DH]
    visible(r2, o2, w2, out_sem.at[1], recv_sem.at[1], back_sem2, True)

    def values(g):
        for h in members(g):
            arrive(w2, back_sem2, h)
        for h in members(g):
            adjoint = w2[2 * h : 2 * h + 2].reshape(LANES, LANES)
            key = kp[h]
            grad = mm(vp[h], adjoint, 1, 1)
            grad = jnp.where(key.astype(jnp.float32) > 0, grad, 0.0)
            dk_ref[:, h * DH : (h + 1) * DH] = grad.astype(jnp.bfloat16)[:, :DH]
            grad = mm(key, adjoint, 1, 0)
            dv_ref[:, h * DH : (h + 1) * DH] = grad.astype(jnp.bfloat16)[:, :DH]

    each_group(values)

    post_end(s1, send_sem.at[0])
    post_end(s2, send_sem.at[1])

    def finish(b, rows):
        drain(o1.at[pl.ds(0, n - 1), pl.ds(0, rows)], out_sem.at[0])
        drain(o2.at[pl.ds(0, n - 1), pl.ds(0, rows)], out_sem.at[1])

    as_owner(finish)


def local(query, key, value, cotangent, labels):
    tokens, width = query.shape
    heads = width // DH
    inner = lax.axis_size("inner")
    n = lax.axis_size("tm") * inner
    units = 2 * heads
    vmem = pl.BlockSpec(memory_space=pltpu.VMEM)
    shape = jax.ShapeDtypeStruct((tokens, width), jnp.bfloat16)
    padded = pltpu.VMEM((heads, tokens, LANES), jnp.bfloat16)
    flat = pltpu.VMEM((tokens, width), jnp.bfloat16)
    per_unit = pltpu.VMEM((units, HALF, LANES), jnp.bfloat16)
    per_device = pltpu.VMEM((n, HALF, LANES), jnp.bfloat16)
    flops = 12 * heads * tokens * DH * DH
    return pl.pallas_call(
        functools.partial(kernel, n, inner, heads),
        out_shape=(shape, shape, shape),
        in_specs=[pl.BlockSpec(memory_space=pltpu.HBM)] * 5,
        out_specs=(vmem, vmem, vmem),
        scratch_shapes=[
            flat, flat, flat, flat, pltpu.VMEM((1, LANES), jnp.int32),
            padded, padded, padded, padded, padded,
            per_unit, per_device, per_device, per_unit,
            per_unit, per_device, per_device, per_unit,
            pltpu.VMEM((n, HALF, LANES), jnp.float32),
            pltpu.SemaphoreType.DMA((5,)),
            pltpu.SemaphoreType.DMA((2, 2)),
            pltpu.SemaphoreType.DMA((2,)),
            pltpu.SemaphoreType.DMA((2,)),
            pltpu.SemaphoreType.DMA((units,)),
            pltpu.SemaphoreType.DMA((units,)),
        ],
        compiler_params=pltpu.CompilerParams(
            collective_id=0, has_side_effects=True, vmem_limit_bytes=63 * 2**20
        ),
        cost_estimate=pl.CostEstimate(
            flops=flops, bytes_accessed=14 * tokens * width, transcendentals=0
        ),
    )(query, key, value, cotangent, labels[:LANES].reshape(1, LANES))


def solution(mesh):
    rows = P(("tm", "inner"), None)
    return jax.shard_map(
        local,
        mesh=mesh,
        in_specs=(rows, rows, rows, rows, P(("tm", "inner"))),
        out_specs=(rows, rows, rows),
        check_vma=False,
    )
```

```python
import functools

import jax
import jax.numpy as jnp
from jax import lax
from jax.experimental import pallas as pl
from jax.experimental.pallas import tpu as pltpu
from jax.sharding import PartitionSpec as P

DH = 112
LANES = 128
HALF = 64
LOSS_SCALE = 1024.0
MASS = DH
LABEL = DH + 1


def mm(a, b, ca, cb):
    return lax.dot_general(
        a, b, (((ca,), (cb,)), ((), ())), preferred_element_type=jnp.float32
    )


GROUPS = 4
ROWS = (HALF, DH - HALF)


def kernel(
    n, inner, heads,
    q_hbm, k_hbm, v_hbm, c_hbm, lab_hbm,
    dq_ref, dk_ref, dv_ref,
    q_ref, k_ref, v_ref, c_ref, lab_ref,
    qp, kp, vp, cp, nb,
    s1, r1, o1, w1, s2, r2, o2, w2, cum,
    in_sem, send_sem, out_sem, recv_sem, back_sem1, back_sem2,
):
    units = 2 * heads
    ratio = n // units
    me = lax.axis_index("tm") * inner + lax.axis_index("inner")
    unit = me // ratio
    per_group = units // GROUPS
    group = unit // per_group
    tokens = q_hbm.shape[0]
    lane_t = lax.broadcasted_iota(jnp.int32, (tokens, LANES), 1)
    lane_s = lax.broadcasted_iota(jnp.int32, (LANES, LANES), 1)

    def place(d):
        return {"tm": d // inner, "inner": d % inner}

    def send(src, dst, d, ssem, rsem):
        pltpu.make_async_remote_copy(
            src_ref=src, dst_ref=dst, send_sem=ssem, recv_sem=rsem,
            device_id=place(d), device_id_type=pl.DeviceIdType.MESH,
        ).start()

    def drain(ref, sem):
        pltpu.make_async_copy(ref, ref, sem).wait()

    fetch = [
        pltpu.make_async_copy(a, b, in_sem.at[i])
        for i, (a, b) in enumerate(
            (
                (lab_hbm, lab_ref), (k_hbm, k_ref), (v_hbm, v_ref),
                (q_hbm, q_ref), (c_hbm, c_ref),
            )
        )
    ]
    for copy in fetch:
        copy.start()

    barrier = pltpu.get_barrier_semaphore()

    def greet(i, carry):
        pl.semaphore_signal(
            barrier, inc=1, device_id=place((me + i) % n),
            device_id_type=pl.DeviceIdType.MESH,
        )
        return carry

    lax.fori_loop(1, n, greet, 0)

    def each_group(fn):
        def step(i, carry):
            now = (group + GROUPS - i) % GROUPS
            for g in range(GROUPS):
                pl.when(now == g)(functools.partial(fn, g))
            return carry

        lax.fori_loop(0, GROUPS, step, 0)

    def post(src, dst, g, ssem, rsem):
        pairs = per_group // 2

        def one(j, carry):
            pair = (unit // 2 + j) % pairs
            for b, rows in enumerate(ROWS):
                u = per_group * g + 2 * pair + b
                here = src.at[u, pl.ds(0, rows)]
                there = dst.at[me, pl.ds(0, rows)]

                @pl.when(u * ratio == me)
                def _():
                    pltpu.make_async_copy(here, there, rsem).start()

                @pl.when(u * ratio != me)
                def _():
                    send(here, there, u * ratio, ssem.at[b], rsem)

            return carry

        lax.fori_loop(0, pairs, one, 0)

    def as_owner(fn):
        for b, rows in enumerate(ROWS):
            mine = unit % 2 == b
            if ratio > 1:
                mine = mine & (me % ratio == 0)
            pl.when(mine)(functools.partial(fn, b, rows))

    def post_end(src, ssem):
        def owner(b, rows):
            for a, size in enumerate(ROWS):
                count = heads - 1 if a == b else heads
                drain(src.at[pl.ds(0, count), pl.ds(0, size)], ssem.at[a])

        as_owner(owner)
        if ratio > 1:

            @pl.when(me % ratio != 0)
            def _():
                for a, size in enumerate(ROWS):
                    drain(src.at[pl.ds(0, heads), pl.ds(0, size)], ssem.at[a])

    def visible(got, out, back, ssem, rsem, bsem, reverse):
        def work(b, rows):
            drain(got.at[pl.ds(0, n), pl.ds(0, rows)], rsem)
            lane_r = lax.broadcasted_iota(jnp.int32, (rows, LANES), 1)

            def add(i, acc):
                d = n - 1 - i if reverse else i
                acc = acc + got[d, :rows].astype(jnp.float32)
                cum[d, :rows] = acc
                return acc

            last = lax.fori_loop(
                0, n, add, jnp.zeros((rows, LANES), jnp.float32), unroll=8
            )

            def label(d):
                column = got[d, :16, LABEL : LABEL + 1].astype(jnp.float32)
                wide = jnp.broadcast_to(column, (16, LANES))
                return jnp.concatenate([wide] * (rows // 16), axis=0)

            def pick(i, carry):
                cur, lab = carry
                d = i if reverse else n - 1 - i
                here = label(d)
                cur = jnp.where(here == lab, cur, cum[d, :rows])
                out[d, :rows] = jnp.where(lane_r == LABEL, 0.0, cur).astype(
                    jnp.bfloat16
                )
                return cur, here

            first = label(0 if reverse else n - 1)
            lax.fori_loop(0, n, pick, (last, first), unroll=8)
            part = pl.ds(0, rows)
            there = back.at[unit, part]
            pltpu.make_async_copy(out.at[me, part], there, bsem.at[unit]).start()
            block = n // GROUPS

            def one(i, carry):
                d = block * ((me // block + i // block) % GROUPS) + (me + i) % block
                send(out.at[d, part], there, d, ssem, bsem.at[unit])
                return carry

            lax.fori_loop(1, n, one, 0)

        as_owner(work)

    def arrive(back, bsem, h):
        for b, rows in enumerate(ROWS):
            u = 2 * h + b
            drain(back.at[u, pl.ds(0, rows)], bsem.at[u])

    zero = jnp.zeros((tokens, LANES), jnp.bfloat16)
    ones = jnp.where(lane_t == MASS, 1.0, 0.0).astype(jnp.bfloat16)
    blank = jnp.zeros((HALF - ROWS[1], LANES), jnp.bfloat16)
    for h in range(heads):
        qp[h] = zero
        kp[h] = zero
        cp[h] = zero
        vp[h] = ones
        w1[2 * h + 1, ROWS[1] :] = blank
        w2[2 * h + 1, ROWS[1] :] = blank
    for copy in fetch[:3]:
        copy.wait()
    lab = jnp.broadcast_to(lab_ref[...].astype(jnp.float32), (LANES, LANES))

    def stage(dst, h, state):
        state = jnp.where(lane_s == LABEL, lab, state).astype(jnp.bfloat16)
        dst[2 * h] = state[:HALF]
        dst[2 * h + 1] = state[HALF:]

    def members(g):
        return range(g * heads // GROUPS, (g + 1) * heads // GROUPS)

    pl.semaphore_wait(barrier, n - 1)

    def keys(g):
        for h in members(g):
            cols = slice(h * DH, (h + 1) * DH)
            kp[h, :, :DH] = jnp.maximum(k_ref[:, cols], 0)
            vp[h, :, :DH] = v_ref[:, cols]
        for h in members(g):
            stage(s1, h, mm(kp[h], vp[h], 0, 0))
        post(s1, r1, g, send_sem.at[0], recv_sem.at[0])

    each_group(keys)

    for copy in fetch[3:]:
        copy.wait()
    for h in range(heads):
        cols = slice(h * DH, (h + 1) * DH)
        qp[h, :, :DH] = jnp.maximum(q_ref[:, cols], 0)
        cp[h, :, :DH] = c_ref[:, cols]
    visible(r1, o1, w1, out_sem.at[0], recv_sem.at[0], back_sem1, False)

    def queries(g):
        for h in members(g):
            arrive(w1, back_sem1, h)
        for h in members(g):
            state = w1[2 * h : 2 * h + 2].reshape(LANES, LANES)
            query = qp[h]
            both = mm(query, state, 1, 0)
            inv = 1.0 / (both[:, MASS : MASS + 1] + float(DH))
            cot = cp[h].astype(jnp.float32) * LOSS_SCALE
            dot = jnp.sum(cot * both, axis=1, keepdims=True)
            back = jnp.where(lane_t == MASS, -(dot * inv) * inv, cot * inv)
            back = back.astype(jnp.bfloat16)
            nb[h] = back
            stage(s2, h, mm(query, back, 0, 0))
        post(s2, r2, g, send_sem.at[1], recv_sem.at[1])

    each_group(queries)

    for h in range(heads):
        state = w1[2 * h : 2 * h + 2].reshape(LANES, LANES)
        grad = mm(nb[h], state, 1, 1)
        grad = jnp.where(qp[h].astype(jnp.float32) > 0, grad, 0.0)
        dq_ref[:, h * DH : (h + 1) * DH] = grad.astype(jnp.bfloat16)[:, :DH]
    visible(r2, o2, w2, out_sem.at[1], recv_sem.at[1], back_sem2, True)

    def values(g):
        for h in members(g):
            arrive(w2, back_sem2, h)
        for h in members(g):
            adjoint = w2[2 * h : 2 * h + 2].reshape(LANES, LANES)
            key = kp[h]
            grad = mm(vp[h], adjoint, 1, 1)
            grad = jnp.where(key.astype(jnp.float32) > 0, grad, 0.0)
            dk_ref[:, h * DH : (h + 1) * DH] = grad.astype(jnp.bfloat16)[:, :DH]
            grad = mm(key, adjoint, 1, 0)
            dv_ref[:, h * DH : (h + 1) * DH] = grad.astype(jnp.bfloat16)[:, :DH]

    each_group(values)

    post_end(s1, send_sem.at[0])
    post_end(s2, send_sem.at[1])

    def finish(b, rows):
        drain(o1.at[pl.ds(0, n - 1), pl.ds(0, rows)], out_sem.at[0])
        drain(o2.at[pl.ds(0, n - 1), pl.ds(0, rows)], out_sem.at[1])

    as_owner(finish)


PIECES = 2


def deliver(*refs):
    sources, results, held, get_sem, put_sem = refs[:3], refs[3:6], *refs[6:]
    rows = sources[0].shape[0] // PIECES
    gets, puts = [], []
    for i in range(3):
        for p in range(PIECES):
            part = pl.ds(p * rows, rows)
            slot = held.at[i, part]
            gets.append(
                pltpu.make_async_copy(sources[i].at[part], slot, get_sem.at[i, p])
            )
            puts.append(
                pltpu.make_async_copy(slot, results[i].at[part], put_sem.at[i, p])
            )
    for copy in gets:
        copy.start()
    for get, put in zip(gets, puts):
        get.wait()
        put.start()
    for copy in puts:
        copy.wait()


def local(query, key, value, cotangent, labels):
    tokens, width = query.shape
    heads = width // DH
    inner = lax.axis_size("inner")
    n = lax.axis_size("tm") * inner
    units = 2 * heads
    vmem = pl.BlockSpec(memory_space=pltpu.VMEM)
    shape = jax.ShapeDtypeStruct((tokens, width), jnp.bfloat16)
    padded = pltpu.VMEM((heads, tokens, LANES), jnp.bfloat16)
    flat = pltpu.VMEM((tokens, width), jnp.bfloat16)
    per_unit = pltpu.VMEM((units, HALF, LANES), jnp.bfloat16)
    per_device = pltpu.VMEM((n, HALF, LANES), jnp.bfloat16)
    flops = 12 * heads * tokens * DH * DH
    grads = pl.pallas_call(
        functools.partial(kernel, n, inner, heads),
        out_shape=(shape, shape, shape),
        in_specs=[pl.BlockSpec(memory_space=pltpu.HBM)] * 5,
        out_specs=(vmem, vmem, vmem),
        scratch_shapes=[
            flat, flat, flat, flat, pltpu.VMEM((1, LANES), jnp.int32),
            padded, padded, padded, padded, padded,
            per_unit, per_device, per_device, per_unit,
            per_unit, per_device, per_device, per_unit,
            pltpu.VMEM((n, HALF, LANES), jnp.float32),
            pltpu.SemaphoreType.DMA((5,)),
            pltpu.SemaphoreType.DMA((2, 2)),
            pltpu.SemaphoreType.DMA((2,)),
            pltpu.SemaphoreType.DMA((2,)),
            pltpu.SemaphoreType.DMA((units,)),
            pltpu.SemaphoreType.DMA((units,)),
        ],
        compiler_params=pltpu.CompilerParams(
            collective_id=0, has_side_effects=True, vmem_limit_bytes=63 * 2**20
        ),
        cost_estimate=pl.CostEstimate(
            flops=flops, bytes_accessed=14 * tokens * width, transcendentals=0
        ),
    )(query, key, value, cotangent, labels[:LANES].reshape(1, LANES))
    hbm = pl.BlockSpec(memory_space=pltpu.HBM)
    return pl.pallas_call(
        deliver,
        out_shape=(shape, shape, shape),
        in_specs=[hbm] * 3,
        out_specs=(hbm, hbm, hbm),
        scratch_shapes=[
            pltpu.VMEM((3, tokens, width), jnp.bfloat16),
            pltpu.SemaphoreType.DMA((3, PIECES)),
            pltpu.SemaphoreType.DMA((3, PIECES)),
        ],
    )(*grads)


def solution(mesh):
    rows = P(("tm", "inner"), None)
    return jax.shard_map(
        local,
        mesh=mesh,
        in_specs=(rows, rows, rows, rows, P(("tm", "inner"))),
        out_specs=(rows, rows, rows),
        check_vma=False,
    )
```
